256 devices in a mesh: seq: 64 (over y, x_hi, z), ch: 4 (over x_lo, core).
Axes of the slice: x: 4 (x_hi: 2, x_lo: 2; x = x_hi * 2 + x_lo), y: 4, z: 8, core: 2. Of those that a mesh axis runs over, the one named last changes fastest.
Arguments:
- streams: bfloat16 [16384, 3, 4096], P(('seq', 'ch')), may hold values from -6 to 6
- filter_taps: float32 [4096, 16384], P('ch', 'seq')
- skip_gain: float32 [4096], P('ch'), may hold values from -1 to 1
Outputs:
- mixed_out: bfloat16 [4096, 16384], P('ch', 'seq')
The draws below stay inside these ranges and needn't reach their ends.
All inputs are finite; a program needn't handle non-finite values.
Results may differ from the reference program's by a relative error of at most 0.001.
Values may be sent and summed in bfloat16 or wider, within the bound.
A program may use at most 128 MiB of HBM per device.

```python
import math
import jax
import jax.numpy as jnp
from jax import lax

C = 4096
SEQUENCE_EXTENT = 16384
SPAN = 32768


def geometric_total(rate):
    return jnp.expm1(-rate * SEQUENCE_EXTENT) / jnp.expm1(-rate)


def draw_filter_taps(key, part):
    key = jax.random.fold_in(key, 7)
    gradual_decay_starter, decay_speed_starter, quick_decay_starter, jitter_random_starter, spike_random_starter, omission_random_starter, floor_random_starter = jax.random.split(key, 7)
    slow_share = 0.5
    slow_pick = jax.random.uniform(gradual_decay_starter, (C, 1)) < slow_share
    slow_rate = jnp.exp(jax.random.uniform(decay_speed_starter, (C, 1), minval=math.log(0.05), maxval=0.0)) * (math.log(10.0) / SEQUENCE_EXTENT)
    fast_rate = jax.random.uniform(quick_decay_starter, (C, 1), minval=1.0 / 50.0, maxval=1.0 / 30.0)
    decay_rate = jnp.where(slow_pick, slow_rate, fast_rate)
    floor_drawn = jax.random.uniform(floor_random_starter, (C, 1), minval=0.04, maxval=0.08)
    floor_weight = jnp.where(slow_pick, 0.0, floor_drawn)
    lags = jnp.arange(SEQUENCE_EXTENT, dtype=jnp.float32)[None, :]
    kernel_decay_profile = jnp.exp(-decay_rate * lags) + floor_weight * jnp.exp(-slow_rate * lags)
    spike_placement_index = jax.random.randint(spike_random_starter, (3,), 1, SEQUENCE_EXTENT)
    spike_retained_mask = jax.random.uniform(omission_random_starter, (3,), minval=0.5, maxval=0.8)
    for chosen_branch_mask in range(3):
        kernel_decay_profile = kernel_decay_profile * jnp.where(jnp.arange(SEQUENCE_EXTENT)[None, :] >= spike_placement_index[chosen_branch_mask], spike_retained_mask[chosen_branch_mask], 1.0)
    scale_sum = geometric_total(2.0 * decay_rate) + 2.0 * floor_weight * geometric_total(decay_rate + slow_rate) + floor_weight * floor_weight * geometric_total(2.0 * slow_rate)
    noise = jax.random.truncated_normal(jitter_random_starter, -6.0, 6.0, (C, SEQUENCE_EXTENT))
    return (noise * kernel_decay_profile / jnp.sqrt(scale_sum)).astype(jnp.float32)


def block_levels(stream_key, extent, pieces, least, high):
    factor_of = 1.0
    for axis_at, blocks in pieces:
        steps = jax.random.uniform(jax.random.fold_in(jax.random.fold_in(stream_key, 6), axis_at), (blocks,), jnp.float32, least / len(pieces), high / len(pieces))
        factor_of = factor_of * jnp.repeat(jnp.exp(steps), extent[axis_at] // blocks).reshape((-1,) + (1,) * (len(extent) - 1 - axis_at))
    return factor_of


def scatter_about(stream_key, extent, deviation, reach, cuts=(), kind=jnp.bfloat16):
    array = deviation * jax.random.normal(stream_key, extent, jnp.float32)
    if cuts:
        array = array * block_levels(stream_key, extent, cuts, -0.22, 0.18)
    return jnp.clip(array, -reach, reach).astype(kind)


def setup_inputs(seed: int = 0) -> dict:
    splits = jax.random.split(jax.random.key(seed), 4)
    return {
        "streams": scatter_about(splits[0], (SEQUENCE_EXTENT, 3, C), 1.0, 6.0, ((0, 256),)),
        "filter_taps": draw_filter_taps(jax.random.fold_in(splits[3], 71), 0),
        "skip_gain": jnp.clip(jax.random.uniform(splits[2], (C,), jnp.float32, -1.0, 1.0) * block_levels(splits[2], (C,), ((0, 4),), -0.4, 0.0), -1.0, 1.0),
    }


def reference(streams, filter_taps, skip_gain):
    group = 256
    count = C // group

    def one_group(index):
        start = (index * group).astype(jnp.int32)
        part = lax.dynamic_slice_in_dim(streams, start, group, 2)
        taps = lax.dynamic_slice_in_dim(filter_taps, start, group, 0)
        gains = lax.dynamic_slice_in_dim(skip_gain, start, group, 0)
        queries = jnp.transpose(part[:, 0, :]).astype(jnp.float32)
        gated_values = jnp.transpose(part[:, 1, :]).astype(jnp.float32) * jnp.transpose(part[:, 2, :]).astype(jnp.float32)
        spectrum = jnp.fft.rfft(gated_values, n=SPAN, axis=1) * jnp.fft.rfft(taps, n=SPAN, axis=1)
        convolved = jnp.fft.irfft(spectrum, n=SPAN, axis=1)[:, :SEQUENCE_EXTENT]
        mixed_sum = convolved + gains[:, None] * gated_values
        return (queries * mixed_sum).astype(jnp.bfloat16)

    result = lax.map(one_group, jnp.arange(count, dtype=jnp.int32))
    return result.reshape(C, SEQUENCE_EXTENT)
```

```python
import functools
import math

import jax
import jax.numpy as jnp
import ml_dtypes
import numpy as np
from jax import lax
from jax.experimental import pallas as pl
from jax.experimental.pallas import tpu as pltpu
from jax.sharding import PartitionSpec as P

MESH = pl.DeviceIdType.MESH
F32 = jnp.float32
BF16 = jnp.bfloat16
R = 128
POWER = 16
TOP = 7.875
FLOOR = 1e-30


def split_np(table):
    high = table.astype(np.float32).astype(ml_dtypes.bfloat16)
    low = (table - high.astype(np.float64)).astype(np.float32).astype(ml_dtypes.bfloat16)
    return high, low


def tables():
    index = np.arange(R, dtype=np.float64)
    theta = (math.pi / 2 + 2 * math.pi * index) / R
    outer = theta[:, None] * index[None, :]
    forward_rows = np.concatenate([np.cos(outer), -np.sin(outer)], 0)
    inverse_rows = np.concatenate([np.cos(outer).T, -np.sin(outer).T], 1)
    twist_re = np.cos(outer / R)
    twist_im = -np.sin(outer / R)
    inner = 2 * math.pi * ((index[:, None] * index[None, :]) % R) / R
    c, s = np.cos(inner), np.sin(inner)
    forward_lanes = np.block([[c, -s], [s, c]])
    inverse_lanes = np.block([[c, s], [-s, c]]) / (R * R)
    mats = []
    for m in (forward_rows, forward_lanes, inverse_lanes, inverse_rows):
        mats.extend(split_np(m))
    twist = np.stack([np.tile(twist_re, (1, 2)), np.tile(twist_im, (1, 2))]).astype(np.float32)
    return mats, twist


def split(x):
    high = x.astype(BF16)
    low = (x - high.astype(F32)).astype(BF16)
    return high, low


def dot(a, b):
    return jnp.dot(a, b, preferred_element_type=F32)


def dot3(a, b):
    return dot(a[0], b[0]) + (dot(a[1], b[0]) + dot(a[0], b[1]))


def scale_of(peak):
    return jnp.log2(jnp.maximum(peak, FLOOR)) - TOP


def encode(x, inverse_scale):
    x = x * inverse_scale
    y = x * x
    y = y * y
    y = y * y
    y = y * y
    return jnp.where(x < 0, -y, y)


def decode(y, log_scale):
    y = y.astype(F32)
    size = jnp.exp2(jnp.log2(jnp.abs(y)) * (1.0 / POWER) + log_scale)
    return jnp.where(y < 0, -size, size)


def kernel(
    streams, taps, skip, f1h, f1l, w2h, w2l, v2h, v2l, i1h, i1l, twist_hbm, out,
    st, hv, gx, gr, qr, qt, sh, rh, eh, reh, sg, rg, eg, reg, so, ro, eo, reo,
    spec, xs, os_, ov, twist, tabs,
    load_sem, gsend, grecv, qsend, qrecv, ssem, rsem,
):
    s = lax.axis_index("seq")
    c = lax.axis_index("ch")
    sz = lax.rem(s, 8)
    sx = lax.rem(s // 8, 2)
    sy = s // 16

    def peer(d):
        y = lax.rem(sy + d // 16, 4)
        x = lax.rem(sx + lax.rem(d // 8, 2), 2)
        z = lax.rem(sz + lax.rem(d, 8), 8)
        return (y * 2 + x) * 8 + z

    barrier = pltpu.get_barrier_semaphore()

    def greet(d, carry):
        pl.semaphore_signal(barrier, inc=1, device_id=(peer(d), c), device_id_type=MESH)
        return carry

    lax.fori_loop(1, 64, greet, 0)
    for d in range(1, 4):
        pl.semaphore_signal(
            barrier, inc=1, device_id=(s, lax.rem(c + d, 4)), device_id_type=MESH
        )

    loads = [
        pltpu.make_async_copy(streams, st, load_sem.at[0]),
        pltpu.make_async_copy(taps, hv, load_sem.at[1]),
        pltpu.make_async_copy(twist_hbm, twist, load_sem.at[2]),
    ]
    for i, source in enumerate((f1h, f1l, w2h, w2l, v2h, v2l, i1h, i1l)):
        loads.append(pltpu.make_async_copy(source, tabs[i], load_sem.at[3 + i]))
    for copy in loads:
        copy.start()

    loads[0].wait()

    def gate(i, carry):
        rows = pl.ds(pl.multiple_of(i * 16, 16), 16)
        gx[rows] = st[1, rows].astype(F32) * st[2, rows].astype(F32)
        return carry

    lax.fori_loop(0, 4, gate, 0)

    def stack_chunks(a, b):
        return jnp.concatenate([a[:, :8], b[:, :8], a[:, 8:], b[:, 8:]], axis=1)

    def encode_group(block, first, send, scales):
        count = block.shape[0] // 16
        block = block.reshape(count, 16, 256)
        a, b = block[:, :, :R], block[:, :, R:]
        peak = jnp.max(jnp.maximum(jnp.abs(a), jnp.abs(b)), axis=1, keepdims=True)
        log_scale = scale_of(peak)
        inverse = jnp.exp2(-log_scale)
        coded = stack_chunks(encode(a, inverse), encode(b, inverse))
        send[pl.ds(first, count)] = coded.astype(BF16)
        scales[pl.ds(first, count)] = log_scale

    loads[1].wait()

    def encode_taps(i, carry):
        encode_group(hv[pl.ds(pl.multiple_of(i * 64, 64), 64), :], i * 4, sh, eh)
        return carry

    lax.fori_loop(0, 16, encode_taps, 0)

    pl.semaphore_wait(barrier, 66)

    mine64 = pl.ds(pl.multiple_of(c * 64, 64), 64)
    copies = []
    for d in (2, 3, 1):
        t = lax.rem(c + d, 4)
        copy = pltpu.make_async_remote_copy(
            gx.at[:, pl.ds(pl.multiple_of(t * 1024, 1024), 1024)],
            gr.at[mine64],
            gsend.at[d - 1],
            grecv.at[d - 1],
            device_id=(s, t),
            device_id_type=MESH,
        )
        copy.start()
        copies.append(copy)

    def send_all(pairs):
        def one(d, carry):
            t = peer(d)
            for source, target, at in pairs:
                pltpu.make_async_remote_copy(
                    source(t), target(s), ssem.at[at], rsem.at[at],
                    device_id=(t, c), device_id_type=MESH,
                ).start()
            return carry

        lax.fori_loop(1, 64, one, 0)

    def whole(ref):
        return lambda i: ref.at[i]

    def half(ref, k):
        return lambda i: ref.at[i, pl.ds(16 * k, 16)]

    def wait_all(ref, sem):
        part = ref.at[pl.ds(0, 63)]
        pltpu.make_async_copy(part, part, sem).wait()

    def wait_half(ref, k, sem):
        part = ref.at[pl.ds(0, 63), pl.ds(16 * k, 16)]
        pltpu.make_async_copy(part, part, sem).wait()

    send_all([(whole(eh), whole(reh), 0), (whole(sh), whole(rh), 1)])
    rh[s] = sh[s]
    reh[s] = eh[s]

    gr[mine64, :] = gx[:, pl.ds(pl.multiple_of(c * 1024, 1024), 1024)]
    for copy in copies:
        copy.wait()

    def encode_gated(j, carry):
        lanes = pl.ds(pl.multiple_of(j * R, R), R)
        encode_group(gr[:, lanes].T, j * 8, sg, eg)
        return carry

    lax.fori_loop(0, 8, encode_gated, 0)

    send_all([(whole(eg), whole(reg), 2), (half(sg, 0), half(rg, 0), 3)])
    send_all([(half(sg, 1), half(rg, 1), 4)])
    rg[s] = sg[s]
    reg[s] = eg[s]

    query_copies = []
    for d in (2, 3, 1):
        t = lax.rem(c + d, 4)
        copy = pltpu.make_async_remote_copy(
            st.at[0, :, pl.ds(pl.multiple_of(t * 1024, 1024), 1024)],
            qr.at[mine64],
            qsend.at[d - 1],
            qrecv.at[d - 1],
            device_id=(s, t),
            device_id_type=MESH,
        )
        copy.start()
        query_copies.append(copy)
    qr[mine64, :] = st[0, :, pl.ds(pl.multiple_of(c * 1024, 1024), 1024)]

    for copy in loads[2:]:
        copy.wait()
    f1 = (tabs[0], tabs[1])
    w2 = (tabs[2], tabs[3])
    v2 = (tabs[4], tabs[5])
    i1 = (tabs[6], tabs[7])

    def get(pair):
        return pair[0][...], pair[1][...]

    def decode_chunk(recv, scales, k):
        def one(i, carry):
            x = decode(recv[pl.ds(i * 4, 4), pl.ds(16 * k, 16)], scales[pl.ds(i * 4, 4)])
            xs[pl.ds(pl.multiple_of(i * 64, 64), 64), :] = x.reshape(64, R)
            return carry

        lax.fori_loop(0, 16, one, 0)

    def forward(p):
        x = jnp.concatenate(
            [xs[pl.ds(2 * p, R, stride=8), :], xs[pl.ds(2 * p + 1, R, stride=8), :]], axis=1
        )
        a = dot3(get(f1), split(x))
        are, aim = a[:R], a[R:]
        tre, tim = twist[0], twist[1]
        bre = are * tre - aim * tim
        bim = are * tim + aim * tre
        rows = jnp.concatenate(
            [
                jnp.concatenate([bre[:, :R], bim[:, :R]], axis=1),
                jnp.concatenate([bre[:, R:], bim[:, R:]], axis=1),
            ],
            axis=0,
        )
        return dot3(split(rows), get(w2))

    wait_all(reh, rsem.at[0])
    wait_all(rh, rsem.at[1])
    for k in range(2):
        decode_chunk(rh, reh, k)

        def transform_taps(p, carry):
            z = forward(p)
            first = s * 16 + 8 * k + 2 * p
            row = lax.broadcasted_iota(jnp.int32, (2 * R, R), 0)
            gain = jnp.where(row < R, skip[first], skip[first + 1])
            spec[k, p] = jnp.concatenate([z[:, :R] + gain, z[:, R:]], axis=1)
            return carry

        lax.fori_loop(0, 4, transform_taps, 0)

    wait_all(reg, rsem.at[2])
    for k in range(2):
        wait_half(rg, k, rsem.at[3 + k])
        decode_chunk(rg, reg, k)

        def convolve(p, carry):
            z = forward(p)
            h = spec[k, p]
            zre, zim, hre, him = z[:, :R], z[:, R:], h[:, :R], h[:, R:]
            prod = jnp.concatenate([zre * hre - zim * him, zre * him + zim * hre], axis=1)
            u = dot3(split(prod), get(v2))
            ure = jnp.concatenate([u[:R, :R], u[R:, :R]], axis=1)
            uim = jnp.concatenate([u[:R, R:], u[R:, R:]], axis=1)
            tre, tim = twist[0], twist[1]
            back = jnp.concatenate([ure * tre + uim * tim, uim * tre - ure * tim], axis=0)
            o = dot3(get(i1), split(back))
            os_[pl.ds(2 * p, R, stride=8), :] = o[:, :R]
            os_[pl.ds(2 * p + 1, R, stride=8), :] = o[:, R:]
            return carry

        lax.fori_loop(0, 4, convolve, 0)

        def encode_result(i, carry):
            x = os_[pl.ds(pl.multiple_of(i * 64, 64), 64), :].reshape(4, 16, R)
            log_scale = scale_of(jnp.max(jnp.abs(x), axis=1, keepdims=True))
            so[k, pl.ds(i * 4, 4)] = encode(x, jnp.exp2(-log_scale)).astype(BF16)
            eo[k, pl.ds(i * 4, 4)] = log_scale
            return carry

        lax.fori_loop(0, 16, encode_result, 0)
        send_all(
            [
                (whole(eo.at[k]), whole(reo.at[k]), 5 + 2 * k),
                (whole(so.at[k]), whole(ro.at[k]), 6 + 2 * k),
            ]
        )
        ro[k, s] = so[k, s]
        reo[k, s] = eo[k, s]
        if k == 0:
            for copy in query_copies:
                copy.wait()

            def turn_queries(j, carry):
                lanes = pl.ds(pl.multiple_of(j * R, R), R)
                rows = pl.ds(pl.multiple_of(j * R, R), R)
                qt[rows, :] = qr[:, lanes].astype(F32).T
                return carry

            lax.fori_loop(0, 8, turn_queries, 0)

    for k in range(2):
        wait_all(reo.at[k], rsem.at[5 + 2 * k])
        wait_all(ro.at[k], rsem.at[6 + 2 * k])

        def finish(i, carry):
            x = decode(ro[k, pl.ds(i * 4, 4)], reo[k, pl.ds(i * 4, 4)])
            x = jnp.concatenate([x[:, :8], x[:, 8:]], axis=2)
            rows = pl.ds(pl.multiple_of(i * 64, 64), 64)
            q = qt[rows, :].reshape(4, 16, 2 * R)
            if k == 0:
                mixed = jnp.concatenate([q[:, :8] * x, q[:, 8:]], axis=1)
                qt[rows, :] = mixed.reshape(64, 2 * R)
            else:
                mixed = jnp.concatenate([q[:, :8], q[:, 8:] * x], axis=1)
                ov[rows, :] = mixed.reshape(64, 2 * R).astype(BF16)
            return carry

        lax.fori_loop(0, 16, finish, 0)

    store = pltpu.make_async_copy(ov, out, load_sem.at[0])
    store.start()
    wait_all(eh, ssem.at[0])
    wait_all(sh, ssem.at[1])
    wait_all(eg, ssem.at[2])
    wait_half(sg, 0, ssem.at[3])
    wait_half(sg, 1, ssem.at[4])
    for k in range(2):
        wait_all(eo.at[k], ssem.at[5 + 2 * k])
        wait_all(so.at[k], ssem.at[6 + 2 * k])
    store.wait()


def body(streams, filter_taps, skip_gain):
    mats, twist = tables()
    streams = jnp.transpose(streams, (1, 0, 2))
    any_spec = pl.BlockSpec(memory_space=pl.ANY)
    dma = pltpu.SemaphoreType.DMA
    vm = pltpu.VMEM
    scratch = [
        vm((3, 64, 4096), BF16),
        vm((1024, 256), F32),
        vm((64, 4096), F32),
        vm((256, 1024), F32),
        vm((256, 1024), BF16),
        vm((1024, 256), F32),
        vm((64, 32, R), BF16),
        vm((64, 32, R), BF16),
        vm((64, 1, R), F32),
        vm((64, 1, R), F32),
        vm((64, 32, R), BF16),
        vm((64, 32, R), BF16),
        vm((64, 1, R), F32),
        vm((64, 1, R), F32),
        vm((2, 64, 16, R), BF16),
        vm((2, 64, 16, R), BF16),
        vm((2, 64, 1, R), F32),
        vm((2, 64, 1, R), F32),
        vm((2, 4, 2 * R, 2 * R), F32),
        vm((1024, R), F32),
        vm((1024, R), F32),
        vm((1024, 256), BF16),
        vm((2, R, 2 * R), F32),
        [vm(m.shape, BF16) for m in mats],
        dma((11,)),
        dma((3,)),
        dma((3,)),
        dma((3,)),
        dma((3,)),
        dma((9,)),
        dma((9,)),
    ]
    return pl.pallas_call(
        kernel,
        out_shape=jax.ShapeDtypeStruct((1024, 256), BF16),
        in_specs=[any_spec, any_spec, pl.BlockSpec(memory_space=pltpu.SMEM)] + [any_spec] * 9,
        out_specs=any_spec,
        scratch_shapes=scratch,
        compiler_params=pltpu.CompilerParams(
            collective_id=0, has_side_effects=True, vmem_limit_bytes=63 * 1024 * 1024
        ),
    )(streams, filter_taps, skip_gain, *[jnp.asarray(m) for m in mats], jnp.asarray(twist))


def solution(mesh):
    placed = (P(("seq", "ch"), None, None), P("ch", "seq"), P("ch"))
    return jax.shard_map(
        body, mesh=mesh, in_specs=placed, out_specs=P("ch", "seq"), check_vma=False
    )
```

```python
import functools
import math

import jax
import jax.numpy as jnp
import ml_dtypes
import numpy as np
from jax import lax
from jax.experimental import pallas as pl
from jax.experimental.pallas import tpu as pltpu
from jax.sharding import PartitionSpec as P

MESH = pl.DeviceIdType.MESH
F32 = jnp.float32
BF16 = jnp.bfloat16
R = 128
POWER = 16
TOP = 7.875
FLOOR = 1e-30


def split_np(table):
    high = table.astype(np.float32).astype(ml_dtypes.bfloat16)
    low = (table - high.astype(np.float64)).astype(np.float32).astype(ml_dtypes.bfloat16)
    return high, low


def tables():
    index = np.arange(R, dtype=np.float64)
    theta = (math.pi / 2 + 2 * math.pi * index) / R
    outer = theta[:, None] * index[None, :]
    forward_rows = np.concatenate([np.cos(outer), -np.sin(outer)], 0)
    inverse_rows = np.concatenate([np.cos(outer).T, -np.sin(outer).T], 1)
    twist_re = np.cos(outer / R)
    twist_im = -np.sin(outer / R)
    inner = 2 * math.pi * ((index[:, None] * index[None, :]) % R) / R
    c, s = np.cos(inner), np.sin(inner)
    forward_lanes = np.block([[c, -s], [s, c]])
    inverse_lanes = np.block([[c, s], [-s, c]]) / (R * R)
    mats = []
    for m, axis in ((forward_rows, 1), (forward_lanes, 0), (inverse_lanes, 0), (inverse_rows, 1)):
        high, low = split_np(m)
        mats.append(np.concatenate([high, high, low], axis))
    twist = np.stack([twist_re, twist_im]).astype(np.float32)
    return mats, twist


def split(x):
    high = x.astype(BF16)
    low = (x - high.astype(F32)).astype(BF16)
    return high, low


def dot(a, b):
    return jnp.dot(a, b, preferred_element_type=F32)


def scale_of(peak):
    return jnp.log2(jnp.maximum(peak, FLOOR)) - TOP


def encode(x, inverse_scale):
    x = x * inverse_scale
    y = x * x
    y = y * y
    y = y * y
    y = y * y
    return jnp.where(x < 0, -y, y)


def decode(y, log_scale):
    y = y.astype(F32)
    size = jnp.exp2(jnp.log2(jnp.abs(y)) * (1.0 / POWER) + log_scale)
    return jnp.where(y < 0, -size, size)


def kernel(
    streams, taps, skip, f1_hbm, w2_hbm, v2_hbm, i1_hbm, twist_hbm, out,
    st, hv, gx, gc, gr, ge, gre, qr, qt, sh, rh, eh, reh, sg, rg, eg, reg, so, ro, eo, reo,
    spec, xs, os_, ov, twist, tabs, wide, first_out, rows3, cols3,
    load_sem, gsend, grecv, gesend, gerecv, qsend, qrecv, ssem, rsem,
):
    s = lax.axis_index("seq")
    c = lax.axis_index("ch")
    sz = lax.rem(s, 8)
    sx = lax.rem(s // 8, 2)
    sy = s // 16

    def peer(d):
        y = lax.rem(sy + d // 16, 4)
        x = lax.rem(sx + lax.rem(d // 8, 2), 2)
        z = lax.rem(sz + lax.rem(d, 8), 8)
        return (y * 2 + x) * 8 + z

    barrier = pltpu.get_barrier_semaphore()

    def greet(d, carry):
        pl.semaphore_signal(barrier, inc=1, device_id=(peer(d), c), device_id_type=MESH)
        return carry

    lax.fori_loop(1, 64, greet, 0)
    for d in range(1, 4):
        pl.semaphore_signal(
            barrier, inc=1, device_id=(s, lax.rem(c + d, 4)), device_id_type=MESH
        )

    loads = [
        pltpu.make_async_copy(streams, st, load_sem.at[0]),
        pltpu.make_async_copy(taps, hv, load_sem.at[1]),
        pltpu.make_async_copy(twist_hbm, twist, load_sem.at[2]),
    ]
    for i, source in enumerate((f1_hbm, w2_hbm, v2_hbm, i1_hbm)):
        loads.append(pltpu.make_async_copy(source, tabs[i], load_sem.at[3 + i]))
    for copy in loads:
        copy.start()

    loads[0].wait()

    def gate(i, peak):
        rows = pl.ds(pl.multiple_of(i * 16, 16), 16)
        g = st[1, rows].astype(F32) * st[2, rows].astype(F32)
        gx[rows] = g
        g = jnp.abs(g)
        return jnp.maximum(peak, jnp.max(jnp.maximum(g[:8], g[8:]).reshape(8, 32, R), axis=1))

    peak = lax.fori_loop(0, 4, gate, jnp.zeros((8, R), F32))
    peak = jnp.max(jnp.max(peak, axis=0, keepdims=True), axis=1, keepdims=True)
    gate_scale = jnp.ceil(scale_of(jnp.broadcast_to(peak, (1, R))))
    ge[...] = gate_scale
    gate_inverse = jnp.exp2(-gate_scale)[:, :1]

    def encode_gate(i, carry):
        rows = pl.ds(pl.multiple_of(i * 16, 16), 16)
        gc[rows] = encode(gx[rows], gate_inverse).astype(BF16)
        return carry

    lax.fori_loop(0, 4, encode_gate, 0)

    def stack_chunks(a, b):
        return jnp.concatenate([a[:, :8], b[:, :8], a[:, 8:], b[:, 8:]], axis=1)

    def encode_group(block, first, send, scales):
        count = block.shape[0] // 16
        block = block.reshape(count, 16, 256)
        a, b = block[:, :, :R], block[:, :, R:]
        peak = jnp.max(jnp.maximum(jnp.abs(a), jnp.abs(b)), axis=1, keepdims=True)
        log_scale = scale_of(peak)
        inverse = jnp.exp2(-log_scale)
        coded = stack_chunks(encode(a, inverse), encode(b, inverse))
        send[pl.ds(first, count)] = coded.astype(BF16)
        scales[pl.ds(first, count)] = log_scale

    loads[1].wait()

    def encode_taps(i, carry):
        encode_group(hv[pl.ds(pl.multiple_of(i * 64, 64), 64), :], i * 4, sh, eh)
        return carry

    lax.fori_loop(0, 16, encode_taps, 0)

    pl.semaphore_wait(barrier, 66)

    mine64 = pl.ds(pl.multiple_of(c * 64, 64), 64)
    copies = []
    for d in (2, 3, 1):
        t = lax.rem(c + d, 4)
        copy = pltpu.make_async_remote_copy(
            ge,
            gre.at[c],
            gesend.at[d - 1],
            gerecv.at[d - 1],
            device_id=(s, t),
            device_id_type=MESH,
        )
        copy.start()
        copies.append(copy)
        copy = pltpu.make_async_remote_copy(
            gc.at[:, pl.ds(pl.multiple_of(t * 1024, 1024), 1024)],
            gr.at[mine64],
            gsend.at[d - 1],
            grecv.at[d - 1],
            device_id=(s, t),
            device_id_type=MESH,
        )
        copy.start()
        copies.append(copy)

    def send_all(pairs):
        def one(d, carry):
            t = peer(d)
            for source, target, at in pairs:
                pltpu.make_async_remote_copy(
                    source(t), target(s), ssem.at[at], rsem.at[at],
                    device_id=(t, c), device_id_type=MESH,
                ).start()
            return carry

        lax.fori_loop(1, 64, one, 0)

    def whole(ref):
        return lambda i: ref.at[i]

    def half(ref, k):
        return lambda i: ref.at[i, pl.ds(16 * k, 16)]

    def wait_all(ref, sem):
        part = ref.at[pl.ds(0, 63)]
        pltpu.make_async_copy(part, part, sem).wait()

    def wait_half(ref, k, sem):
        part = ref.at[pl.ds(0, 63), pl.ds(16 * k, 16)]
        pltpu.make_async_copy(part, part, sem).wait()

    send_all([(whole(eh), whole(reh), 0), (half(sh, 0), half(rh, 0), 1)])
    send_all([(half(sh, 1), half(rh, 1), 9)])
    rh[s] = sh[s]
    reh[s] = eh[s]

    gr[mine64, :] = gc[:, pl.ds(pl.multiple_of(c * 1024, 1024), 1024)]
    gre[c] = ge[...]
    for copy in copies:
        copy.wait()

    parts = gre[...]
    common = jnp.max(parts, axis=0)
    factor = jnp.exp2((parts - common[None]) * POWER)
    eg[...] = jnp.broadcast_to(common[None], eg.shape)

    def encode_gated(j, carry):
        lanes = pl.ds(pl.multiple_of(j * R, R), R)
        x = gr[:, lanes].astype(F32).reshape(4, 64, R) * factor
        x = x.reshape(256, R).T.reshape(8, 16, 256)
        sg[pl.ds(j * 8, 8)] = stack_chunks(x[:, :, :R], x[:, :, R:]).astype(BF16)
        return carry

    lax.fori_loop(0, 8, encode_gated, 0)

    send_all([(whole(eg), whole(reg), 2), (half(sg, 0), half(rg, 0), 3)])
    rg[s] = sg[s]
    reg[s] = eg[s]

    for copy in loads[2:]:
        copy.wait()
    f1, w2, v2, i1 = tabs

    def decode_chunk(recv, scales, k):
        def one(i, carry):
            x = decode(recv[pl.ds(i * 4, 4), pl.ds(16 * k, 16)], scales[pl.ds(i * 4, 4)])
            xs[pl.ds(pl.multiple_of(i * 64, 64), 64), :] = x.reshape(64, R)
            return carry

        lax.fori_loop(0, 16, one, 0)

    def put_rows(at, x):
        high, low = split(x)
        rows3[at, 0:256] = high
        rows3[at, 256:512] = low
        rows3[at, 512:768] = high

    def forward():
        x = jnp.concatenate([xs[pl.ds(q, R, stride=8), :] for q in range(8)], axis=1)
        high, low = split(x)
        wide[0:R] = high
        wide[R : 2 * R] = low
        wide[2 * R : 3 * R] = high
        first_out[...] = dot(f1[...], wide[...])
        tre, tim = twist[0], twist[1]
        for q in range(8):
            lanes = pl.ds(q * R, R)
            are, aim = first_out[0:R, lanes], first_out[R : 2 * R, lanes]
            both = jnp.concatenate([are * tre - aim * tim, are * tim + aim * tre], axis=1)
            put_rows(pl.ds(q * R, R), both)

    def transform_taps(k):
        forward()
        for p in range(4):
            z = dot(rows3[pl.ds(p * 256, 256), :], w2[...])
            first = s * 16 + 8 * k + 2 * p
            row = lax.broadcasted_iota(jnp.int32, (2 * R, R), 0)
            gain = jnp.where(row < R, skip[first], skip[first + 1])
            spec[k, p] = jnp.concatenate([z[:, :R] + gain, z[:, R:]], axis=1)

    def convolve(k):
        forward()
        for p in range(4):
            rows = pl.ds(p * 256, 256)
            z = dot(rows3[rows, :], w2[...])
            h = spec[k, p]
            zre, zim, hre, him = z[:, :R], z[:, R:], h[:, :R], h[:, R:]
            put_rows(rows, jnp.concatenate([zre * hre - zim * him, zre * him + zim * hre], axis=1))
        tre, tim = twist[0], twist[1]
        for p in range(4):
            u = dot(rows3[pl.ds(p * 256, 256), :], v2[...])
            for q in range(2):
                ure, uim = u[q * R : (q + 1) * R, :R], u[q * R : (q + 1) * R, R:]
                back = jnp.concatenate([ure * tre + uim * tim, uim * tre - ure * tim], axis=0)
                high, low = split(back)
                lanes = pl.ds((2 * p + q) * R, R)
                cols3[0:256, lanes] = high
                cols3[256:512, lanes] = low
                cols3[512:768, lanes] = high
        o = dot(i1[...], cols3[...])
        for q in range(8):
            os_[pl.ds(q, R, stride=8), :] = o[:, q * R : (q + 1) * R]

    wait_all(reh, rsem.at[0])
    for k in range(2):
        wait_half(rh, k, rsem.at[1 + 8 * k])
        decode_chunk(rh, reh, k)

        transform_taps(k)
        if k == 0:
            send_all([(half(sg, 1), half(rg, 1), 4)])
            query_copies = []
            for d in (2, 3, 1):
                t = lax.rem(c + d, 4)
                copy = pltpu.make_async_remote_copy(
                    st.at[0, :, pl.ds(pl.multiple_of(t * 1024, 1024), 1024)],
                    qr.at[mine64],
                    qsend.at[d - 1],
                    qrecv.at[d - 1],
                    device_id=(s, t),
                    device_id_type=MESH,
                )
                copy.start()
                query_copies.append(copy)
            qr[mine64, :] = st[0, :, pl.ds(pl.multiple_of(c * 1024, 1024), 1024)]

    wait_all(reg, rsem.at[2])
    for k in range(2):
        wait_half(rg, k, rsem.at[3 + k])
        decode_chunk(rg, reg, k)

        convolve(k)

        def encode_result(i, carry):
            x = os_[pl.ds(pl.multiple_of(i * 64, 64), 64), :].reshape(4, 16, R)
            log_scale = scale_of(jnp.max(jnp.abs(x), axis=1, keepdims=True))
            so[k, pl.ds(i * 4, 4)] = encode(x, jnp.exp2(-log_scale)).astype(BF16)
            eo[k, pl.ds(i * 4, 4)] = log_scale
            return carry

        lax.fori_loop(0, 16, encode_result, 0)
        send_all(
            [
                (whole(eo.at[k]), whole(reo.at[k]), 5 + 2 * k),
                (whole(so.at[k]), whole(ro.at[k]), 6 + 2 * k),
            ]
        )
        ro[k, s] = so[k, s]
        reo[k, s] = eo[k, s]
        if k == 0:
            for copy in query_copies:
                copy.wait()

            def turn_queries(j, carry):
                lanes = pl.ds(pl.multiple_of(j * R, R), R)
                rows = pl.ds(pl.multiple_of(j * R, R), R)
                qt[rows, :] = qr[:, lanes].astype(F32).T
                return carry

            lax.fori_loop(0, 8, turn_queries, 0)

    for k in range(2):
        wait_all(reo.at[k], rsem.at[5 + 2 * k])
        wait_all(ro.at[k], rsem.at[6 + 2 * k])

        def finish(i, carry):
            x = decode(ro[k, pl.ds(i * 4, 4)], reo[k, pl.ds(i * 4, 4)])
            x = jnp.concatenate([x[:, :8], x[:, 8:]], axis=2)
            rows = pl.ds(pl.multiple_of(i * 64, 64), 64)
            q = qt[rows, :].reshape(4, 16, 2 * R)
            if k == 0:
                mixed = jnp.concatenate([q[:, :8] * x, q[:, 8:]], axis=1)
                qt[rows, :] = mixed.reshape(64, 2 * R)
            else:
                mixed = jnp.concatenate([q[:, :8], q[:, 8:] * x], axis=1)
                ov[rows, :] = mixed.reshape(64, 2 * R).astype(BF16)
            return carry

        lax.fori_loop(0, 16, finish, 0)

    store = pltpu.make_async_copy(ov, out, load_sem.at[0])
    store.start()
    wait_all(eh, ssem.at[0])
    wait_half(sh, 0, ssem.at[1])
    wait_half(sh, 1, ssem.at[9])
    wait_all(eg, ssem.at[2])
    wait_half(sg, 0, ssem.at[3])
    wait_half(sg, 1, ssem.at[4])
    for k in range(2):
        wait_all(eo.at[k], ssem.at[5 + 2 * k])
        wait_all(so.at[k], ssem.at[6 + 2 * k])
    store.wait()


def body(streams, filter_taps, skip_gain):
    mats, twist = tables()
    streams = jnp.transpose(streams, (1, 0, 2))
    any_spec = pl.BlockSpec(memory_space=pl.ANY)
    dma = pltpu.SemaphoreType.DMA
    vm = pltpu.VMEM
    scratch = [
        vm((3, 64, 4096), BF16),
        vm((1024, 256), F32),
        vm((64, 4096), F32),
        vm((64, 4096), BF16),
        vm((256, 1024), BF16),
        vm((1, R), F32),
        vm((4, 1, R), F32),
        vm((256, 1024), BF16),
        vm((1024, 256), F32),
        vm((64, 32, R), BF16),
        vm((64, 32, R), BF16),
        vm((64, 1, R), F32),
        vm((64, 1, R), F32),
        vm((64, 32, R), BF16),
        vm((64, 32, R), BF16),
        vm((64, 1, R), F32),
        vm((64, 1, R), F32),
        vm((2, 64, 16, R), BF16),
        vm((2, 64, 16, R), BF16),
        vm((2, 64, 1, R), F32),
        vm((2, 64, 1, R), F32),
        vm((2, 4, 2 * R, 2 * R), F32),
        vm((1024, R), F32),
        vm((1024, R), F32),
        vm((1024, 256), BF16),
        vm((2, R, R), F32),
        [vm(m.shape, BF16) for m in mats],
        vm((3 * R, 8 * R), BF16),
        vm((2 * R, 8 * R), F32),
        vm((8 * R, 6 * R), BF16),
        vm((6 * R, 8 * R), BF16),
        dma((7,)),
        dma((3,)),
        dma((3,)),
        dma((3,)),
        dma((3,)),
        dma((3,)),
        dma((3,)),
        dma((10,)),
        dma((10,)),
    ]
    return pl.pallas_call(
        kernel,
        out_shape=jax.ShapeDtypeStruct((1024, 256), BF16),
        in_specs=[any_spec, any_spec, pl.BlockSpec(memory_space=pltpu.SMEM)] + [any_spec] * 5,
        out_specs=any_spec,
        scratch_shapes=scratch,
        compiler_params=pltpu.CompilerParams(
            collective_id=0, has_side_effects=True, vmem_limit_bytes=63 * 1024 * 1024
        ),
    )(streams, filter_taps, skip_gain, *[jnp.asarray(m) for m in mats], jnp.asarray(twist))


def solution(mesh):
    placed = (P(("seq", "ch"), None, None), P("ch", "seq"), P("ch"))
    return jax.shard_map(
        body, mesh=mesh, in_specs=placed, out_specs=P("ch", "seq"), check_vma=False
    )
```

```python
import functools
import math

import jax
import jax.numpy as jnp
import ml_dtypes
import numpy as np
from jax import lax
from jax.experimental import pallas as pl
from jax.experimental.pallas import tpu as pltpu
from jax.sharding import PartitionSpec as P

MESH = pl.DeviceIdType.MESH
F32 = jnp.float32
BF16 = jnp.bfloat16
R = 128
POWER = 16
TOP = 7.875
FLOOR = 1e-30


def split_np(table):
    high = table.astype(np.float32).astype(ml_dtypes.bfloat16)
    low = (table - high.astype(np.float64)).astype(np.float32).astype(ml_dtypes.bfloat16)
    return high, low


def tables():
    index = np.arange(R, dtype=np.float64)
    theta = (math.pi / 2 + 2 * math.pi * index) / R
    outer = theta[:, None] * index[None, :]
    forward_rows = np.concatenate([np.cos(outer), -np.sin(outer)], 0)
    inverse_rows = np.concatenate([np.cos(outer).T, -np.sin(outer).T], 1)
    twist_re = np.cos(outer / R)
    twist_im = -np.sin(outer / R)
    inner = 2 * math.pi * ((index[:, None] * index[None, :]) % R) / R
    c, s = np.cos(inner), np.sin(inner)
    forward_lanes = np.block([[c, -s], [s, c]])
    inverse_lanes = np.block([[c, s], [-s, c]]) / (R * R)
    mats = []
    for m, axis in ((forward_rows, 1), (forward_lanes, 0), (inverse_lanes, 0), (inverse_rows, 1)):
        high, low = split_np(m)
        mats.append(np.concatenate([high, high, low], axis))
    twist = np.stack([twist_re, twist_im]).astype(np.float32)
    return mats, twist


def split(x):
    high = x.astype(BF16)
    low = (x - high.astype(F32)).astype(BF16)
    return high, low


def dot(a, b):
    return jnp.dot(a, b, preferred_element_type=F32)


def scale_of(peak):
    return jnp.log2(jnp.maximum(peak, FLOOR)) - TOP


def encode(x, inverse_scale):
    x = x * inverse_scale
    y = x * x
    y = y * y
    y = y * y
    y = y * y
    return jnp.where(x < 0, -y, y)


def decode(y, log_scale):
    y = y.astype(F32)
    size = jnp.exp2(jnp.log2(jnp.abs(y)) * (1.0 / POWER) + log_scale)
    return jnp.where(y < 0, -size, size)


def kernel(
    streams, taps, skip, f1_hbm, w2_hbm, v2_hbm, i1_hbm, twist_hbm, out,
    st, hv, gx, gc, gr, ge, gre, qr, qt, sh, rh, eh, reh, sg, rg, eg, reg, so, ro, eo, reo,
    spec, xs, os_, twist, tabs, wide, first_out, rows3, cols3,
    load_sem, gsend, grecv, gesend, gerecv, qsend, qrecv, ssem, rsem, scsend, screcv,
):
    s = lax.axis_index("seq")
    c = lax.axis_index("ch")
    sz = lax.rem(s, 8)
    sx = lax.rem(s // 8, 2)
    sy = s // 16

    def peer(d):
        y = lax.rem(sy + d // 16, 4)
        x = lax.rem(sx + lax.rem(d // 8, 2), 2)
        z = lax.rem(sz + lax.rem(d, 8), 8)
        return (y * 2 + x) * 8 + z

    barrier = pltpu.get_barrier_semaphore()

    def greet(d, carry):
        pl.semaphore_signal(barrier, inc=1, device_id=(peer(d), c), device_id_type=MESH)
        return carry

    lax.fori_loop(1, 64, greet, 0)
    for d in range(1, 4):
        pl.semaphore_signal(
            barrier, inc=1, device_id=(s, lax.rem(c + d, 4)), device_id_type=MESH
        )

    loads = [
        pltpu.make_async_copy(taps, hv, load_sem.at[0]),
        pltpu.make_async_copy(streams, st, load_sem.at[1]),
        pltpu.make_async_copy(twist_hbm, twist, load_sem.at[2]),
    ]
    for i, source in enumerate((f1_hbm, w2_hbm, v2_hbm, i1_hbm)):
        loads.append(pltpu.make_async_copy(source, tabs[i], load_sem.at[3 + i]))
    for copy in loads:
        copy.start()

    def stack_chunks(a, b):
        return jnp.concatenate([a[:, :8], b[:, :8], a[:, 8:], b[:, 8:]], axis=1)

    loads[0].wait()

    def peak_taps(i, peak):
        block = jnp.abs(hv[pl.ds(pl.multiple_of(i * 64, 64), 64), :])
        block = jnp.maximum(block[:, :R], block[:, R:])
        return jnp.maximum(peak, jnp.max(block.reshape(8, 8, R), axis=0))

    peak = lax.fori_loop(0, 16, peak_taps, jnp.zeros((8, R), F32))
    tap_scale = scale_of(jnp.max(peak, axis=0, keepdims=True))
    eh[...] = tap_scale
    tap_inverse = jnp.exp2(-tap_scale)

    def encode_taps(i, carry):
        block = hv[pl.ds(pl.multiple_of(i * 64, 64), 64), :]
        a = encode(block[:, :R], tap_inverse).reshape(4, 16, R)
        b = encode(block[:, R:], tap_inverse).reshape(4, 16, R)
        sh[pl.ds(i * 4, 4)] = stack_chunks(a, b).astype(BF16)
        return carry

    lax.fori_loop(0, 16, encode_taps, 0)

    loads[1].wait()

    def gate(i, peak):
        rows = pl.ds(pl.multiple_of(i * 16, 16), 16)
        g = st[1, rows].astype(F32) * st[2, rows].astype(F32)
        gx[rows] = g
        g = jnp.abs(g)
        return jnp.maximum(peak, jnp.max(jnp.maximum(g[:8], g[8:]).reshape(8, 32, R), axis=1))

    peak = lax.fori_loop(0, 4, gate, jnp.zeros((8, R), F32))
    peak = jnp.max(jnp.max(peak, axis=0, keepdims=True), axis=1, keepdims=True)
    gate_scale = jnp.ceil(scale_of(jnp.broadcast_to(peak, (1, R))))
    ge[...] = gate_scale
    gate_inverse = jnp.exp2(-gate_scale)[:, :1]

    def encode_gate(i, carry):
        rows = pl.ds(pl.multiple_of(i * 16, 16), 16)
        gc[rows] = encode(gx[rows], gate_inverse).astype(BF16)
        return carry

    lax.fori_loop(0, 4, encode_gate, 0)

    pl.semaphore_wait(barrier, 66)

    def send_all(pairs):
        def one(d, carry):
            t = peer(d)
            for source, target, at in pairs:
                pltpu.make_async_remote_copy(
                    source(t), target(s), ssem.at[at], rsem.at[at],
                    device_id=(t, c), device_id_type=MESH,
                ).start()
            return carry

        lax.fori_loop(1, 64, one, 0)

    def whole(ref):
        return lambda i: ref.at[i]

    def half(ref, k):
        return lambda i: ref.at[i, pl.ds(16 * k, 16)]

    def wait_all(ref, sem):
        part = ref.at[pl.ds(0, 63)]
        pltpu.make_async_copy(part, part, sem).wait()

    def wait_half(ref, k, sem):
        part = ref.at[pl.ds(0, 63), pl.ds(16 * k, 16)]
        pltpu.make_async_copy(part, part, sem).wait()

    block = s // 8
    same_block = pl.ds(pl.multiple_of(block * 8, 8), 8)

    def share_lines(row, rows, at):
        for d in range(1, 8):
            pltpu.make_async_remote_copy(
                row, rows.at[s], scsend.at[2 * at], screcv.at[2 * at],
                device_id=(block * 8 + lax.rem(sz + d, 8), c), device_id_type=MESH,
            ).start()
        rows[s] = row[...]

    def wait_rows(rows, count, sem):
        part = rows.at[pl.ds(0, count)]
        pltpu.make_async_copy(part, part, sem).wait()

    def share_blocks(rows, at):
        wait_rows(rows, 7, screcv.at[2 * at])
        for d in range(1, 8):
            pltpu.make_async_remote_copy(
                rows.at[same_block], rows.at[same_block], scsend.at[2 * at + 1], screcv.at[2 * at + 1],
                device_id=(lax.rem(block + d, 8) * 8 + sz, c), device_id_type=MESH,
            ).start()

    def wait_scales(rows, at):
        wait_rows(rows, 56, screcv.at[2 * at + 1])

    mine64 = pl.ds(pl.multiple_of(c * 64, 64), 64)
    copies = []
    for d in (2, 3, 1):
        t = lax.rem(c + d, 4)
        copy = pltpu.make_async_remote_copy(
            ge,
            gre.at[c],
            gesend.at[d - 1],
            gerecv.at[d - 1],
            device_id=(s, t),
            device_id_type=MESH,
        )
        copy.start()
        copies.append(copy)
        copy = pltpu.make_async_remote_copy(
            gc.at[:, pl.ds(pl.multiple_of(t * 1024, 1024), 1024)],
            gr.at[mine64],
            gsend.at[d - 1],
            grecv.at[d - 1],
            device_id=(s, t),
            device_id_type=MESH,
        )
        copy.start()
        copies.append(copy)

    share_lines(eh, reh, 0)
    send_all([(half(sh, 0), half(rh, 0), 0)])
    send_all([(half(sh, 1), half(rh, 1), 1)])
    rh[s] = sh[s]

    gr[mine64, :] = gc[:, pl.ds(pl.multiple_of(c * 1024, 1024), 1024)]
    gre[c] = ge[...]
    for copy in copies:
        copy.wait()

    parts = gre[...]
    common = jnp.max(parts, axis=0)
    factor = jnp.exp2((parts - common[None]) * POWER)
    eg[...] = common
    share_lines(eg, reg, 1)

    def encode_gated(j, carry):
        lanes = pl.ds(pl.multiple_of(j * R, R), R)
        x = gr[:, lanes].astype(F32).reshape(4, 64, R) * factor
        x = x.reshape(256, R).T.reshape(8, 16, 256)
        sg[pl.ds(j * 8, 8)] = stack_chunks(x[:, :, :R], x[:, :, R:]).astype(BF16)
        return carry

    lax.fori_loop(0, 8, encode_gated, 0)

    send_all([(half(sg, 0), half(rg, 0), 2)])
    share_blocks(reh, 0)
    share_blocks(reg, 1)
    send_all([(half(sg, 1), half(rg, 1), 3)])
    rg[s] = sg[s]

    for copy in loads[2:]:
        copy.wait()
    f1, w2, v2, i1 = tabs

    def decode_chunk(recv, scales, k):
        def one(i, carry):
            x = decode(recv[pl.ds(i * 4, 4), pl.ds(16 * k, 16)], scales[pl.ds(i * 4, 4)])
            xs[pl.ds(pl.multiple_of(i * 64, 64), 64), :] = x.reshape(64, R)
            return carry

        lax.fori_loop(0, 16, one, 0)

    def put_rows(at, x):
        high, low = split(x)
        rows3[at, 0:256] = high
        rows3[at, 256:512] = low
        rows3[at, 512:768] = high

    def forward():
        x = jnp.concatenate([xs[pl.ds(q, R, stride=8), :] for q in range(8)], axis=1)
        high, low = split(x)
        wide[0:R] = high
        wide[R : 2 * R] = low
        wide[2 * R : 3 * R] = high
        first_out[...] = dot(f1[...], wide[...])
        tre, tim = twist[0], twist[1]
        for q in range(8):
            lanes = pl.ds(q * R, R)
            are, aim = first_out[0:R, lanes], first_out[R : 2 * R, lanes]
            both = jnp.concatenate([are * tre - aim * tim, are * tim + aim * tre], axis=1)
            put_rows(pl.ds(q * R, R), both)

    def transform_taps(k):
        forward()
        for p in range(4):
            z = dot(rows3[pl.ds(p * 256, 256), :], w2[...])
            first = s * 16 + 8 * k + 2 * p
            row = lax.broadcasted_iota(jnp.int32, (2 * R, R), 0)
            gain = jnp.where(row < R, skip[first], skip[first + 1])
            spec[k, p] = jnp.concatenate([z[:, :R] + gain, z[:, R:]], axis=1)

    def convolve(k):
        forward()
        for p in range(4):
            rows = pl.ds(p * 256, 256)
            z = dot(rows3[rows, :], w2[...])
            h = spec[k, p]
            zre, zim, hre, him = z[:, :R], z[:, R:], h[:, :R], h[:, R:]
            put_rows(rows, jnp.concatenate([zre * hre - zim * him, zre * him + zim * hre], axis=1))
        tre, tim = twist[0], twist[1]
        for p in range(4):
            u = dot(rows3[pl.ds(p * 256, 256), :], v2[...])
            for q in range(2):
                ure, uim = u[q * R : (q + 1) * R, :R], u[q * R : (q + 1) * R, R:]
                back = jnp.concatenate([ure * tre + uim * tim, uim * tre - ure * tim], axis=0)
                high, low = split(back)
                lanes = pl.ds((2 * p + q) * R, R)
                cols3[0:256, lanes] = high
                cols3[256:512, lanes] = low
                cols3[512:768, lanes] = high
        o = dot(i1[...], cols3[...])
        for q in range(8):
            os_[pl.ds(q, R, stride=8), :] = o[:, q * R : (q + 1) * R]

    wait_scales(reh, 0)
    for k in range(2):
        wait_half(rh, k, rsem.at[k])
        decode_chunk(rh, reh, k)

        transform_taps(k)
        if k == 0:
            query_copies = []
            for d in (2, 3, 1):
                t = lax.rem(c + d, 4)
                copy = pltpu.make_async_remote_copy(
                    st.at[0, :, pl.ds(pl.multiple_of(t * 1024, 1024), 1024)],
                    qr.at[mine64],
                    qsend.at[d - 1],
                    qrecv.at[d - 1],
                    device_id=(s, t),
                    device_id_type=MESH,
                )
                copy.start()
                query_copies.append(copy)
            qr[mine64, :] = st[0, :, pl.ds(pl.multiple_of(c * 1024, 1024), 1024)]

    wait_scales(reg, 1)
    for k in range(2):
        wait_half(rg, k, rsem.at[2 + k])
        decode_chunk(rg, reg, k)

        convolve(k)

        def peak_result(i, peak):
            x = jnp.abs(os_[pl.ds(pl.multiple_of(i * 64, 64), 64), :])
            return jnp.maximum(peak, jnp.max(x.reshape(8, 8, R), axis=0))

        peak = lax.fori_loop(0, 16, peak_result, jnp.zeros((8, R), F32))
        log_scale = scale_of(jnp.max(peak, axis=0, keepdims=True))
        eo[k] = log_scale
        share_lines(eo.at[k], reo.at[k], 2 + k)
        inverse = jnp.exp2(-log_scale)

        def encode_result(i, carry):
            x = encode(os_[pl.ds(pl.multiple_of(i * 64, 64), 64), :], inverse)
            so[k, pl.ds(i * 4, 4)] = x.reshape(4, 16, R).astype(BF16)
            return carry

        lax.fori_loop(0, 16, encode_result, 0)
        send_all([(whole(so.at[k]), whole(ro.at[k]), 4 + k)])
        ro[k, s] = so[k, s]
        if k == 0:
            for copy in query_copies:
                copy.wait()

            def turn_queries(j, carry):
                lanes = pl.ds(pl.multiple_of(j * R, R), R)
                rows = pl.ds(pl.multiple_of(j * R, R), R)
                qt[rows, :] = qr[:, lanes].astype(F32).T
                return carry

            lax.fori_loop(0, 8, turn_queries, 0)
            share_blocks(reo.at[0], 2)

    share_blocks(reo.at[1], 3)
    for k in range(2):
        wait_scales(reo.at[k], 2 + k)
        wait_all(ro.at[k], rsem.at[4 + k])

        def finish(i, carry):
            x = decode(ro[k, pl.ds(i * 4, 4)], reo[k, pl.ds(i * 4, 4)])
            x = jnp.concatenate([x[:, :8], x[:, 8:]], axis=2)
            rows = pl.ds(pl.multiple_of(i * 64, 64), 64)
            q = qt[rows, :].reshape(4, 16, 2 * R)
            if k == 0:
                mixed = jnp.concatenate([q[:, :8] * x, q[:, 8:]], axis=1)
                qt[rows, :] = mixed.reshape(64, 2 * R)
            else:
                mixed = jnp.concatenate([q[:, :8], q[:, 8:] * x], axis=1)
                out[rows, :] = mixed.reshape(64, 2 * R).astype(BF16)
            return carry

        lax.fori_loop(0, 16, finish, 0)

    for k in range(2):
        wait_half(sh, k, ssem.at[k])
        wait_half(sg, k, ssem.at[2 + k])
        wait_all(so.at[k], ssem.at[4 + k])
    for i, rows in enumerate((reh, reg, reo.at[0], reo.at[1])):
        wait_rows(rows, 7, scsend.at[2 * i])
        wait_rows(rows, 56, scsend.at[2 * i + 1])


def body(streams, filter_taps, skip_gain):
    mats, twist = tables()
    streams = jnp.transpose(streams, (1, 0, 2))
    any_spec = pl.BlockSpec(memory_space=pltpu.HBM)
    dma = pltpu.SemaphoreType.DMA
    vm = pltpu.VMEM
    scratch = [
        vm((3, 64, 4096), BF16),
        vm((1024, 256), F32),
        vm((64, 4096), F32),
        vm((64, 4096), BF16),
        vm((256, 1024), BF16),
        vm((1, R), F32),
        vm((4, 1, R), F32),
        vm((256, 1024), BF16),
        vm((1024, 256), F32),
        vm((64, 32, R), BF16),
        vm((64, 32, R), BF16),
        vm((1, R), F32),
        vm((64, 1, R), F32),
        vm((64, 32, R), BF16),
        vm((64, 32, R), BF16),
        vm((1, R), F32),
        vm((64, 1, R), F32),
        vm((2, 64, 16, R), BF16),
        vm((2, 64, 16, R), BF16),
        vm((2, 1, R), F32),
        vm((2, 64, 1, R), F32),
        vm((2, 4, 2 * R, 2 * R), F32),
        vm((1024, R), F32),
        vm((1024, R), F32),
        vm((2, R, R), F32),
        [vm(m.shape, BF16) for m in mats],
        vm((3 * R, 8 * R), BF16),
        vm((2 * R, 8 * R), F32),
        vm((8 * R, 6 * R), BF16),
        vm((6 * R, 8 * R), BF16),
        dma((7,)),
        dma((3,)),
        dma((3,)),
        dma((3,)),
        dma((3,)),
        dma((3,)),
        dma((3,)),
        dma((6,)),
        dma((6,)),
        dma((8,)),
        dma((8,)),
    ]
    return pl.pallas_call(
        kernel,
        out_shape=pltpu.VMEM((1024, 256), BF16),
        in_specs=[any_spec, any_spec, pl.BlockSpec(memory_space=pltpu.SMEM)] + [any_spec] * 5,
        out_specs=pl.BlockSpec(memory_space=pltpu.VMEM),
        scratch_shapes=scratch,
        compiler_params=pltpu.CompilerParams(
            collective_id=0, has_side_effects=True, vmem_limit_bytes=63 * 1024 * 1024
        ),
    )(streams, filter_taps, skip_gain, *[jnp.asarray(m) for m in mats], jnp.asarray(twist))


def solution(mesh):
    placed = (P(("seq", "ch"), None, None), P("ch", "seq"), P("ch"))
    return jax.shard_map(
        body, mesh=mesh, in_specs=placed, out_specs=P("ch", "seq"), check_vma=False
    )
```

```python
import functools
import math

import jax
import jax.numpy as jnp
import ml_dtypes
import numpy as np
from jax import lax
from jax.experimental import pallas as pl
from jax.experimental.pallas import tpu as pltpu
from jax.sharding import PartitionSpec as P

MESH = pl.DeviceIdType.MESH
F32 = jnp.float32
BF16 = jnp.bfloat16
R = 128
POWER = 16
TOP = 7.875
FLOOR = 1e-30


def split_np(table):
    high = table.astype(np.float32).astype(ml_dtypes.bfloat16)
    low = (table - high.astype(np.float64)).astype(np.float32).astype(ml_dtypes.bfloat16)
    return high, low


def tables():
    index = np.arange(R, dtype=np.float64)
    theta = (math.pi / 2 + 2 * math.pi * index) / R
    outer = theta[:, None] * index[None, :]
    forward_rows = np.concatenate([np.cos(outer), -np.sin(outer)], 0)
    inverse_rows = np.concatenate([np.cos(outer).T, -np.sin(outer).T], 1)
    twist_re = np.cos(outer / R)
    twist_im = -np.sin(outer / R)
    inner = 2 * math.pi * ((index[:, None] * index[None, :]) % R) / R
    c, s = np.cos(inner), np.sin(inner)
    forward_lanes = np.block([[c, -s], [s, c]])
    inverse_lanes = np.block([[c, s], [-s, c]]) / (R * R)
    mats = []
    for m, axis in ((forward_rows, 1), (forward_lanes, 0), (inverse_lanes, 0), (inverse_rows, 1)):
        high, low = split_np(m)
        mats.append(np.concatenate([high, high, low], axis))
    twist = np.stack([twist_re, twist_im]).astype(np.float32)
    return mats, twist


def split(x):
    high = x.astype(BF16)
    low = (x - high.astype(F32)).astype(BF16)
    return high, low


def dot(a, b):
    return jnp.dot(a, b, preferred_element_type=F32)


def scale_of(peak):
    return jnp.log2(jnp.maximum(peak, FLOOR)) - TOP


def encode(x, inverse_scale):
    x = x * inverse_scale
    y = x * x
    y = y * y
    y = y * y
    y = y * y
    return jnp.where(x < 0, -y, y)


def decode(y, log_scale):
    y = y.astype(F32)
    size = jnp.exp2(jnp.log2(jnp.abs(y)) * (1.0 / POWER) + log_scale)
    return jnp.where(y < 0, -size, size)


def kernel(
    streams, taps, skip, f1_hbm, w2_hbm, v2_hbm, i1_hbm, twist_hbm, out,
    st, hv, gx, gc, gr, ge, gre, qr, qt, sh, rh, eh, reh, sg, rg, eg, reg, so, ro, eo, reo,
    spec, xs, os_, twist, tabs, wide, first_out, rows3, cols3,
    load_sem, gsend, grecv, gesend, gerecv, qsend, qrecv, ssem, rsem, scsend, screcv,
):
    s = lax.axis_index("seq")
    c = lax.axis_index("ch")
    sz = lax.rem(s, 8)
    sx = lax.rem(s // 8, 2)
    sy = s // 16

    def peer(d):
        y = lax.rem(sy + d // 16, 4)
        x = lax.rem(sx + lax.rem(d // 8, 2), 2)
        z = lax.rem(sz + lax.rem(d, 8), 8)
        return (y * 2 + x) * 8 + z

    barrier = pltpu.get_barrier_semaphore()

    def greet(d, carry):
        pl.semaphore_signal(barrier, inc=1, device_id=(peer(d), c), device_id_type=MESH)
        return carry

    lax.fori_loop(1, 64, greet, 0)
    for d in range(1, 4):
        pl.semaphore_signal(
            barrier, inc=1, device_id=(s, lax.rem(c + d, 4)), device_id_type=MESH
        )

    loads = [
        pltpu.make_async_copy(taps, hv, load_sem.at[0]),
        pltpu.make_async_copy(streams, st, load_sem.at[1]),
        pltpu.make_async_copy(twist_hbm, twist, load_sem.at[2]),
    ]
    for i, source in enumerate((f1_hbm, w2_hbm, v2_hbm, i1_hbm)):
        loads.append(pltpu.make_async_copy(source, tabs[i], load_sem.at[3 + i]))
    for copy in loads:
        copy.start()

    def stack_chunks(a, b):
        return jnp.concatenate([a[:, :8], b[:, :8], a[:, 8:], b[:, 8:]], axis=1)

    loads[0].wait()

    def peak_taps(i, peak):
        block = jnp.abs(hv[pl.ds(pl.multiple_of(i * 64, 64), 64), :])
        block = jnp.maximum(block[:, :R], block[:, R:])
        return jnp.maximum(peak, jnp.max(block.reshape(8, 8, R), axis=0))

    peak = lax.fori_loop(0, 16, peak_taps, jnp.zeros((8, R), F32))
    tap_scale = scale_of(jnp.max(peak, axis=0, keepdims=True))
    eh[...] = tap_scale
    tap_inverse = jnp.exp2(-tap_scale)

    def encode_taps(i, carry):
        block = hv[pl.ds(pl.multiple_of(i * 64, 64), 64), :]
        a = encode(block[:, :R], tap_inverse).reshape(4, 16, R)
        b = encode(block[:, R:], tap_inverse).reshape(4, 16, R)
        sh[pl.ds(i * 4, 4)] = stack_chunks(a, b).astype(BF16)
        return carry

    lax.fori_loop(0, 16, encode_taps, 0)

    loads[1].wait()

    def gate(i, peak):
        rows = pl.ds(pl.multiple_of(i * 16, 16), 16)
        g = st[1, rows].astype(F32) * st[2, rows].astype(F32)
        gx[rows] = g
        g = jnp.abs(g)
        return jnp.maximum(peak, jnp.max(jnp.maximum(g[:8], g[8:]).reshape(8, 32, R), axis=1))

    peak = lax.fori_loop(0, 4, gate, jnp.zeros((8, R), F32))
    peak = jnp.max(jnp.max(peak, axis=0, keepdims=True), axis=1, keepdims=True)
    gate_scale = jnp.ceil(scale_of(jnp.broadcast_to(peak, (1, R))))
    ge[...] = gate_scale
    gate_inverse = jnp.exp2(-gate_scale)[:, :1]

    def encode_gate(i, carry):
        rows = pl.ds(pl.multiple_of(i * 16, 16), 16)
        gc[rows] = encode(gx[rows], gate_inverse).astype(BF16)
        return carry

    lax.fori_loop(0, 4, encode_gate, 0)

    pl.semaphore_wait(barrier, 66)

    def send_all(pairs):
        def one(d, carry):
            t = peer(d)
            for source, target, at in pairs:
                pltpu.make_async_remote_copy(
                    source(t), target(s), ssem.at[at], rsem.at[at],
                    device_id=(t, c), device_id_type=MESH,
                ).start()
            return carry

        lax.fori_loop(1, 64, one, 0)

    def whole(ref):
        return lambda i: ref.at[i]

    def half(ref, k):
        return lambda i: ref.at[i, pl.ds(16 * k, 16)]

    def wait_all(ref, sem):
        part = ref.at[pl.ds(0, 63)]
        pltpu.make_async_copy(part, part, sem).wait()

    def wait_half(ref, k, sem):
        part = ref.at[pl.ds(0, 63), pl.ds(16 * k, 16)]
        pltpu.make_async_copy(part, part, sem).wait()

    block = s // 8
    same_block = pl.ds(pl.multiple_of(block * 8, 8), 8)

    def share_lines(row, rows, at):
        for d in range(1, 8):
            pltpu.make_async_remote_copy(
                row, rows.at[s], scsend.at[2 * at], screcv.at[2 * at],
                device_id=(block * 8 + lax.rem(sz + d, 8), c), device_id_type=MESH,
            ).start()
        rows[s] = row[...]

    def wait_rows(rows, count, sem):
        part = rows.at[pl.ds(0, count)]
        pltpu.make_async_copy(part, part, sem).wait()

    def share_blocks(rows, at):
        wait_rows(rows, 7, screcv.at[2 * at])
        for d in range(1, 8):
            pltpu.make_async_remote_copy(
                rows.at[same_block], rows.at[same_block], scsend.at[2 * at + 1], screcv.at[2 * at + 1],
                device_id=(lax.rem(block + d, 8) * 8 + sz, c), device_id_type=MESH,
            ).start()

    def wait_scales(rows, at):
        wait_rows(rows, 56, screcv.at[2 * at + 1])

    mine64 = pl.ds(pl.multiple_of(c * 64, 64), 64)
    copies = []
    for d in (2, 3, 1):
        t = lax.rem(c + d, 4)
        copy = pltpu.make_async_remote_copy(
            ge,
            gre.at[c],
            gesend.at[d - 1],
            gerecv.at[d - 1],
            device_id=(s, t),
            device_id_type=MESH,
        )
        copy.start()
        copies.append(copy)
        copy = pltpu.make_async_remote_copy(
            gc.at[:, pl.ds(pl.multiple_of(t * 1024, 1024), 1024)],
            gr.at[mine64],
            gsend.at[d - 1],
            grecv.at[d - 1],
            device_id=(s, t),
            device_id_type=MESH,
        )
        copy.start()
        copies.append(copy)

    share_lines(eh, reh, 0)
    send_all([(half(sh, 0), half(rh, 0), 0)])
    send_all([(half(sh, 1), half(rh, 1), 1)])
    rh[s] = sh[s]

    gr[mine64, :] = gc[:, pl.ds(pl.multiple_of(c * 1024, 1024), 1024)]
    gre[c] = ge[...]
    for copy in copies:
        copy.wait()

    parts = gre[...]
    common = jnp.max(parts, axis=0)
    factor = jnp.exp2((parts - common[None]) * POWER)
    eg[...] = common
    share_lines(eg, reg, 1)

    def encode_gated(j, carry):
        lanes = pl.ds(pl.multiple_of(j * R, R), R)
        x = gr[:, lanes].astype(F32).reshape(4, 64, R) * factor
        x = x.reshape(256, R).T.reshape(8, 16, 256)
        sg[pl.ds(j * 8, 8)] = stack_chunks(x[:, :, :R], x[:, :, R:]).astype(BF16)
        return carry

    lax.fori_loop(0, 8, encode_gated, 0)

    send_all([(half(sg, 0), half(rg, 0), 2)])
    share_blocks(reh, 0)
    share_blocks(reg, 1)
    send_all([(half(sg, 1), half(rg, 1), 3)])
    rg[s] = sg[s]

    for copy in loads[2:]:
        copy.wait()
    f1, w2, v2, i1 = tabs

    def decode_chunk(recv, scales, k):
        def one(i, carry):
            x = decode(recv[pl.ds(i * 4, 4), pl.ds(16 * k, 16)], scales[pl.ds(i * 4, 4)])
            xs[pl.ds(pl.multiple_of(i * 64, 64), 64), :] = x.reshape(64, R)
            return carry

        lax.fori_loop(0, 16, one, 0)

    def put_rows(at, x):
        high, low = split(x)
        rows3[at, 0:256] = high
        rows3[at, 256:512] = low
        rows3[at, 512:768] = high

    def forward():
        x = jnp.concatenate([xs[pl.ds(q, R, stride=8), :] for q in range(8)], axis=1)
        high, low = split(x)
        wide[0:R] = high
        wide[R : 2 * R] = low
        wide[2 * R : 3 * R] = high
        first_out[...] = dot(f1[...], wide[...])
        tre, tim = twist[0], twist[1]
        for q in range(8):
            lanes = pl.ds(q * R, R)
            are, aim = first_out[0:R, lanes], first_out[R : 2 * R, lanes]
            both = jnp.concatenate([are * tre - aim * tim, are * tim + aim * tre], axis=1)
            put_rows(pl.ds(q * R, R), both)

    def transform_taps(k):
        forward()
        for p in range(4):
            z = dot(rows3[pl.ds(p * 256, 256), :], w2[...])
            first = s * 16 + 8 * k + 2 * p
            row = lax.broadcasted_iota(jnp.int32, (2 * R, R), 0)
            gain = jnp.where(row < R, skip[first], skip[first + 1])
            spec[k, p] = jnp.concatenate([z[:, :R] + gain, z[:, R:]], axis=1)

    def convolve(k):
        forward()
        for p in range(4):
            rows = pl.ds(p * 256, 256)
            z = dot(rows3[rows, :], w2[...])
            h = spec[k, p]
            zre, zim, hre, him = z[:, :R], z[:, R:], h[:, :R], h[:, R:]
            put_rows(rows, jnp.concatenate([zre * hre - zim * him, zre * him + zim * hre], axis=1))
        tre, tim = twist[0], twist[1]
        for p in range(4):
            u = dot(rows3[pl.ds(p * 256, 256), :], v2[...])
            for q in range(2):
                ure, uim = u[q * R : (q + 1) * R, :R], u[q * R : (q + 1) * R, R:]
                back = jnp.concatenate([ure * tre + uim * tim, uim * tre - ure * tim], axis=0)
                high, low = split(back)
                lanes = pl.ds((2 * p + q) * R, R)
                cols3[0:256, lanes] = high
                cols3[256:512, lanes] = low
                cols3[512:768, lanes] = high
        o = dot(i1[...], cols3[...])
        for q in range(8):
            os_[pl.ds(q, R, stride=8), :] = o[:, q * R : (q + 1) * R]

    wait_scales(reh, 0)
    for k in range(2):
        wait_half(rh, k, rsem.at[k])
        decode_chunk(rh, reh, k)

        transform_taps(k)
        if k == 0:
            query_copies = []
            for d in (2, 3, 1):
                t = lax.rem(c + d, 4)
                copy = pltpu.make_async_remote_copy(
                    st.at[0, :, pl.ds(pl.multiple_of(t * 1024, 1024), 1024)],
                    qr.at[mine64],
                    qsend.at[d - 1],
                    qrecv.at[d - 1],
                    device_id=(s, t),
                    device_id_type=MESH,
                )
                copy.start()
                query_copies.append(copy)
            qr[mine64, :] = st[0, :, pl.ds(pl.multiple_of(c * 1024, 1024), 1024)]

    wait_scales(reg, 1)
    for k in range(2):
        wait_half(rg, k, rsem.at[2 + k])
        decode_chunk(rg, reg, k)

        convolve(k)

        def peak_result(i, peak):
            x = jnp.abs(os_[pl.ds(pl.multiple_of(i * 64, 64), 64), :])
            return jnp.maximum(peak, jnp.max(x.reshape(8, 8, R), axis=0))

        peak = lax.fori_loop(0, 16, peak_result, jnp.zeros((8, R), F32))
        log_scale = scale_of(jnp.max(peak, axis=0, keepdims=True))
        eo[k] = log_scale
        share_lines(eo.at[k], reo.at[k], 2 + k)
        inverse = jnp.exp2(-log_scale)

        def encode_result(i, carry):
            x = encode(os_[pl.ds(pl.multiple_of(i * 64, 64), 64), :], inverse)
            so[k, pl.ds(i * 4, 4)] = x.reshape(4, 16, R).astype(BF16)
            return carry

        lax.fori_loop(0, 16, encode_result, 0)
        send_all([(whole(so.at[k]), whole(ro.at[k]), 4 + k)])
        ro[k, s] = so[k, s]
        if k == 0:
            share_blocks(reo.at[0], 2)

    for copy in query_copies:
        copy.wait()

    def turn_queries(j, carry):
        lanes = pl.ds(pl.multiple_of(j * R, R), R)
        rows = pl.ds(pl.multiple_of(j * R, R), R)
        qt[rows, :] = qr[:, lanes].astype(F32).T
        return carry

    lax.fori_loop(0, 8, turn_queries, 0)
    share_blocks(reo.at[1], 3)
    for k in range(2):
        wait_scales(reo.at[k], 2 + k)
        wait_all(ro.at[k], rsem.at[4 + k])

        def finish(i, carry):
            x = decode(ro[k, pl.ds(i * 4, 4)], reo[k, pl.ds(i * 4, 4)])
            x = jnp.concatenate([x[:, :8], x[:, 8:]], axis=2)
            rows = pl.ds(pl.multiple_of(i * 64, 64), 64)
            q = qt[rows, :].reshape(4, 16, 2 * R)
            if k == 0:
                mixed = jnp.concatenate([q[:, :8] * x, q[:, 8:]], axis=1)
                qt[rows, :] = mixed.reshape(64, 2 * R)
            else:
                mixed = jnp.concatenate([q[:, :8], q[:, 8:] * x], axis=1)
                out[rows, :] = mixed.reshape(64, 2 * R).astype(BF16)
            return carry

        lax.fori_loop(0, 16, finish, 0)

    for k in range(2):
        wait_half(sh, k, ssem.at[k])
        wait_half(sg, k, ssem.at[2 + k])
        wait_all(so.at[k], ssem.at[4 + k])
    for i, rows in enumerate((reh, reg, reo.at[0], reo.at[1])):
        wait_rows(rows, 7, scsend.at[2 * i])
        wait_rows(rows, 56, scsend.at[2 * i + 1])


def body(streams, filter_taps, skip_gain):
    mats, twist = tables()
    streams = jnp.transpose(streams, (1, 0, 2))
    any_spec = pl.BlockSpec(memory_space=pltpu.HBM)
    dma = pltpu.SemaphoreType.DMA
    vm = pltpu.VMEM
    scratch = [
        vm((3, 64, 4096), BF16),
        vm((1024, 256), F32),
        vm((64, 4096), F32),
        vm((64, 4096), BF16),
        vm((256, 1024), BF16),
        vm((1, R), F32),
        vm((4, 1, R), F32),
        vm((256, 1024), BF16),
        vm((1024, 256), F32),
        vm((64, 32, R), BF16),
        vm((64, 32, R), BF16),
        vm((1, R), F32),
        vm((64, 1, R), F32),
        vm((64, 32, R), BF16),
        vm((64, 32, R), BF16),
        vm((1, R), F32),
        vm((64, 1, R), F32),
        vm((2, 64, 16, R), BF16),
        vm((2, 64, 16, R), BF16),
        vm((2, 1, R), F32),
        vm((2, 64, 1, R), F32),
        vm((2, 4, 2 * R, 2 * R), F32),
        vm((1032, R), F32),
        vm((1032, R), F32),
        vm((2, R, R), F32),
        [vm(m.shape, BF16) for m in mats],
        vm((3 * R, 8 * R), BF16),
        vm((2 * R, 8 * R), F32),
        vm((8 * R, 6 * R), BF16),
        vm((6 * R, 8 * R), BF16),
        dma((7,)),
        dma((3,)),
        dma((3,)),
        dma((3,)),
        dma((3,)),
        dma((3,)),
        dma((3,)),
        dma((6,)),
        dma((6,)),
        dma((8,)),
        dma((8,)),
    ]
    return pl.pallas_call(
        kernel,
        out_shape=pltpu.VMEM((1024, 256), BF16),
        in_specs=[any_spec, any_spec, pl.BlockSpec(memory_space=pltpu.SMEM)] + [any_spec] * 5,
        out_specs=pl.BlockSpec(memory_space=pltpu.VMEM),
        scratch_shapes=scratch,
        compiler_params=pltpu.CompilerParams(
            collective_id=0, has_side_effects=True, vmem_limit_bytes=63 * 1024 * 1024
        ),
    )(streams, filter_taps, skip_gain, *[jnp.asarray(m) for m in mats], jnp.asarray(twist))


def solution(mesh):
    placed = (P(("seq", "ch"), None, None), P("ch", "seq"), P("ch"))
    return jax.shard_map(
        body, mesh=mesh, in_specs=placed, out_specs=P("ch", "seq"), check_vma=False
    )
```

```python
import functools
import math

import jax
import jax.numpy as jnp
import ml_dtypes
import numpy as np
from jax import lax
from jax.experimental import pallas as pl
from jax.experimental.pallas import tpu as pltpu
from jax.sharding import PartitionSpec as P

MESH = pl.DeviceIdType.MESH
F32 = jnp.float32
BF16 = jnp.bfloat16
R = 128
POWER = 16
TOP = 7.875
FLOOR = 1e-30


def split_np(table):
    high = table.astype(np.float32).astype(ml_dtypes.bfloat16)
    low = (table - high.astype(np.float64)).astype(np.float32).astype(ml_dtypes.bfloat16)
    return high, low


def tables():
    index = np.arange(R, dtype=np.float64)
    theta = (math.pi / 2 + 2 * math.pi * index) / R
    outer = theta[:, None] * index[None, :]
    forward_rows = np.concatenate([np.cos(outer), -np.sin(outer)], 0)
    inverse_rows = np.concatenate([np.cos(outer).T, -np.sin(outer).T], 1)
    twist_re = np.cos(outer / R)
    twist_im = -np.sin(outer / R)
    inner = 2 * math.pi * ((index[:, None] * index[None, :]) % R) / R
    c, s = np.cos(inner), np.sin(inner)
    forward_lanes = np.block([[c, -s], [s, c]])
    inverse_lanes = np.block([[c, s], [-s, c]]) / (R * R)
    mats = []
    for m, axis in ((forward_rows, 1), (forward_lanes, 0), (inverse_lanes, 0), (inverse_rows, 1)):
        high, low = split_np(m)
        mats.append(np.concatenate([high, high, low], axis))
    twist = np.stack([twist_re, twist_im]).astype(np.float32)
    return mats, twist


def split(x):
    high = x.astype(BF16)
    low = (x - high.astype(F32)).astype(BF16)
    return high, low


def dot(a, b):
    return jnp.dot(a, b, preferred_element_type=F32)


def scale_of(peak):
    return jnp.log2(jnp.maximum(peak, FLOOR)) - TOP


def encode(x, inverse_scale):
    x = x * inverse_scale
    y = x * x
    y = y * y
    y = y * y
    y = y * y
    return jnp.where(x < 0, -y, y)


def decode(y, log_scale):
    y = y.astype(F32)
    size = jnp.exp2(jnp.log2(jnp.abs(y)) * (1.0 / POWER) + log_scale)
    return jnp.where(y < 0, -size, size)


def kernel(
    streams, taps, skip, f1_hbm, w2_hbm, v2_hbm, i1_hbm, twist_hbm, out,
    st, hv, gx, gc, gr, ge, gre, qr, qt, sh, rh, eh, reh, sg, rg, eg, reg, so, ro, eo, reo,
    spec, xs, os_, twist, tabs, wide, first_out, rows3, cols3,
    load_sem, gsend, grecv, gesend, gerecv, qsend, qrecv, ssem, rsem, scsend, screcv,
):
    s = lax.axis_index("seq")
    c = lax.axis_index("ch")
    sz = lax.rem(s, 8)
    sx = lax.rem(s // 8, 2)
    sy = s // 16

    def peer(d):
        y = lax.rem(sy + d // 16, 4)
        x = lax.rem(sx + lax.rem(d // 8, 2), 2)
        z = lax.rem(sz + lax.rem(d, 8), 8)
        return (y * 2 + x) * 8 + z

    barrier = pltpu.get_barrier_semaphore()

    def greet(d, carry):
        pl.semaphore_signal(barrier, inc=1, device_id=(peer(d), c), device_id_type=MESH)
        return carry

    lax.fori_loop(1, 64, greet, 0)
    for d in range(1, 4):
        pl.semaphore_signal(
            barrier, inc=1, device_id=(s, lax.rem(c + d, 4)), device_id_type=MESH
        )

    loads = [
        pltpu.make_async_copy(taps, hv, load_sem.at[0]),
        pltpu.make_async_copy(streams, st, load_sem.at[1]),
        pltpu.make_async_copy(twist_hbm, twist, load_sem.at[2]),
    ]
    for i, source in enumerate((f1_hbm, w2_hbm, v2_hbm, i1_hbm)):
        loads.append(pltpu.make_async_copy(source, tabs[i], load_sem.at[3 + i]))
    for copy in loads:
        copy.start()

    def stack_chunks(a, b):
        return jnp.concatenate([a[:, :8], b[:, :8], a[:, 8:], b[:, 8:]], axis=1)

    loads[0].wait()

    def peak_taps(i, peak):
        block = jnp.abs(hv[pl.ds(pl.multiple_of(i * 64, 64), 64), :])
        block = jnp.maximum(block[:, :R], block[:, R:])
        return jnp.maximum(peak, jnp.max(block.reshape(8, 8, R), axis=0))

    peak = lax.fori_loop(0, 16, peak_taps, jnp.zeros((8, R), F32))
    tap_scale = scale_of(jnp.max(peak, axis=0, keepdims=True))
    eh[...] = tap_scale
    tap_inverse = jnp.exp2(-tap_scale)

    def encode_taps(i, carry):
        block = hv[pl.ds(pl.multiple_of(i * 64, 64), 64), :]
        a = encode(block[:, :R], tap_inverse).reshape(4, 16, R)
        b = encode(block[:, R:], tap_inverse).reshape(4, 16, R)
        sh[pl.ds(i * 4, 4)] = stack_chunks(a, b).astype(BF16)
        return carry

    lax.fori_loop(0, 16, encode_taps, 0)

    loads[1].wait()

    def gate(i, peak):
        rows = pl.ds(pl.multiple_of(i * 16, 16), 16)
        g = st[1, rows].astype(F32) * st[2, rows].astype(F32)
        gx[rows] = g
        g = jnp.abs(g)
        return jnp.maximum(peak, jnp.max(jnp.maximum(g[:8], g[8:]).reshape(8, 32, R), axis=1))

    peak = lax.fori_loop(0, 4, gate, jnp.zeros((8, R), F32))
    peak = jnp.max(jnp.max(peak, axis=0, keepdims=True), axis=1, keepdims=True)
    gate_scale = jnp.ceil(scale_of(jnp.broadcast_to(peak, (1, R))))
    ge[...] = gate_scale
    gate_inverse = jnp.exp2(-gate_scale)[:, :1]

    def encode_gate(i, carry):
        rows = pl.ds(pl.multiple_of(i * 16, 16), 16)
        gc[rows] = encode(gx[rows], gate_inverse).astype(BF16)
        return carry

    lax.fori_loop(0, 4, encode_gate, 0)

    pl.semaphore_wait(barrier, 66)

    def send_all(pairs):
        def one(d, carry):
            t = peer(d)
            for source, target, at in pairs:
                pltpu.make_async_remote_copy(
                    source(t), target(s), ssem.at[at], rsem.at[at],
                    device_id=(t, c), device_id_type=MESH,
                ).start()
            return carry

        lax.fori_loop(1, 64, one, 0)

    def whole(ref):
        return lambda i: ref.at[i]

    def half(ref, k):
        return lambda i: ref.at[i, pl.ds(16 * k, 16)]

    def wait_all(ref, sem):
        part = ref.at[pl.ds(0, 63)]
        pltpu.make_async_copy(part, part, sem).wait()

    def wait_half(ref, k, sem):
        part = ref.at[pl.ds(0, 63), pl.ds(16 * k, 16)]
        pltpu.make_async_copy(part, part, sem).wait()

    block = s // 8
    same_block = pl.ds(pl.multiple_of(block * 8, 8), 8)

    def share_lines(row, rows, at):
        for d in range(1, 8):
            pltpu.make_async_remote_copy(
                row, rows.at[s], scsend.at[2 * at], screcv.at[2 * at],
                device_id=(block * 8 + lax.rem(sz + d, 8), c), device_id_type=MESH,
            ).start()
        rows[s] = row[...]

    def wait_rows(rows, count, sem):
        part = rows.at[pl.ds(0, count)]
        pltpu.make_async_copy(part, part, sem).wait()

    def share_blocks(rows, at):
        wait_rows(rows, 7, screcv.at[2 * at])
        for d in range(1, 8):
            pltpu.make_async_remote_copy(
                rows.at[same_block], rows.at[same_block], scsend.at[2 * at + 1], screcv.at[2 * at + 1],
                device_id=(lax.rem(block + d, 8) * 8 + sz, c), device_id_type=MESH,
            ).start()

    def wait_scales(rows, at):
        wait_rows(rows, 56, screcv.at[2 * at + 1])

    mine64 = pl.ds(pl.multiple_of(c * 64, 64), 64)
    copies = []
    for d in (2, 3, 1):
        t = lax.rem(c + d, 4)
        copy = pltpu.make_async_remote_copy(
            ge,
            gre.at[c],
            gesend.at[d - 1],
            gerecv.at[d - 1],
            device_id=(s, t),
            device_id_type=MESH,
        )
        copy.start()
        copies.append(copy)
        copy = pltpu.make_async_remote_copy(
            gc.at[:, pl.ds(pl.multiple_of(t * 1024, 1024), 1024)],
            gr.at[mine64],
            gsend.at[d - 1],
            grecv.at[d - 1],
            device_id=(s, t),
            device_id_type=MESH,
        )
        copy.start()
        copies.append(copy)

    share_lines(eh, reh, 0)
    send_all([(half(sh, 0), half(rh, 0), 0)])
    send_all([(half(sh, 1), half(rh, 1), 1)])
    rh[s] = sh[s]

    gr[mine64, :] = gc[:, pl.ds(pl.multiple_of(c * 1024, 1024), 1024)]
    gre[c] = ge[...]
    for copy in copies:
        copy.wait()

    parts = gre[...]
    common = jnp.max(parts, axis=0)
    factor = jnp.exp2((parts - common[None]) * POWER)
    eg[...] = common
    share_lines(eg, reg, 1)

    def encode_gated(j, carry):
        lanes = pl.ds(pl.multiple_of(j * R, R), R)
        x = gr[:, lanes].astype(F32).reshape(4, 64, R) * factor
        x = x.reshape(256, R).T.reshape(8, 16, 256)
        sg[pl.ds(j * 8, 8)] = stack_chunks(x[:, :, :R], x[:, :, R:]).astype(BF16)
        return carry

    lax.fori_loop(0, 8, encode_gated, 0, unroll=2)

    send_all([(half(sg, 0), half(rg, 0), 2)])
    share_blocks(reh, 0)
    share_blocks(reg, 1)
    send_all([(half(sg, 1), half(rg, 1), 3)])
    rg[s] = sg[s]

    for copy in loads[2:]:
        copy.wait()
    f1, w2, v2, i1 = tabs

    def decode_chunk(recv, scales, k):
        def one(i, carry):
            x = decode(recv[pl.ds(i * 4, 4), pl.ds(16 * k, 16)], scales[pl.ds(i * 4, 4)])
            xs[pl.ds(pl.multiple_of(i * 64, 64), 64), :] = x.reshape(64, R)
            return carry

        lax.fori_loop(0, 16, one, 0, unroll=2)

    def put_rows(at, x):
        high, low = split(x)
        rows3[at, 0:256] = high
        rows3[at, 256:512] = low
        rows3[at, 512:768] = high

    def forward():
        x = jnp.concatenate([xs[pl.ds(q, R, stride=8), :] for q in range(8)], axis=1)
        high, low = split(x)
        wide[0:R] = high
        wide[R : 2 * R] = low
        wide[2 * R : 3 * R] = high
        first_out[...] = dot(f1[...], wide[...])
        tre, tim = twist[0], twist[1]
        for q in range(8):
            lanes = pl.ds(q * R, R)
            are, aim = first_out[0:R, lanes], first_out[R : 2 * R, lanes]
            both = jnp.concatenate([are * tre - aim * tim, are * tim + aim * tre], axis=1)
            put_rows(pl.ds(q * R, R), both)

    def transform_taps(k):
        forward()
        for p in range(4):
            z = dot(rows3[pl.ds(p * 256, 256), :], w2[...])
            first = s * 16 + 8 * k + 2 * p
            row = lax.broadcasted_iota(jnp.int32, (2 * R, R), 0)
            gain = jnp.where(row < R, skip[first], skip[first + 1])
            spec[k, p] = jnp.concatenate([z[:, :R] + gain, z[:, R:]], axis=1)

    def convolve(k):
        forward()
        for p in range(4):
            rows = pl.ds(p * 256, 256)
            z = dot(rows3[rows, :], w2[...])
            h = spec[k, p]
            zre, zim, hre, him = z[:, :R], z[:, R:], h[:, :R], h[:, R:]
            put_rows(rows, jnp.concatenate([zre * hre - zim * him, zre * him + zim * hre], axis=1))
        tre, tim = twist[0], twist[1]
        for p in range(4):
            u = dot(rows3[pl.ds(p * 256, 256), :], v2[...])
            for q in range(2):
                ure, uim = u[q * R : (q + 1) * R, :R], u[q * R : (q + 1) * R, R:]
                back = jnp.concatenate([ure * tre + uim * tim, uim * tre - ure * tim], axis=0)
                high, low = split(back)
                lanes = pl.ds((2 * p + q) * R, R)
                cols3[0:256, lanes] = high
                cols3[256:512, lanes] = low
                cols3[512:768, lanes] = high
        o = dot(i1[...], cols3[...])
        for q in range(8):
            os_[pl.ds(q, R, stride=8), :] = o[:, q * R : (q + 1) * R]

    wait_scales(reh, 0)
    for k in range(2):
        wait_half(rh, k, rsem.at[k])
        decode_chunk(rh, reh, k)

        transform_taps(k)
        if k == 0:
            query_copies = []
            for d in (2, 3, 1):
                t = lax.rem(c + d, 4)
                copy = pltpu.make_async_remote_copy(
                    st.at[0, :, pl.ds(pl.multiple_of(t * 1024, 1024), 1024)],
                    qr.at[mine64],
                    qsend.at[d - 1],
                    qrecv.at[d - 1],
                    device_id=(s, t),
                    device_id_type=MESH,
                )
                copy.start()
                query_copies.append(copy)
            qr[mine64, :] = st[0, :, pl.ds(pl.multiple_of(c * 1024, 1024), 1024)]

    wait_scales(reg, 1)
    for k in range(2):
        wait_half(rg, k, rsem.at[2 + k])
        decode_chunk(rg, reg, k)

        convolve(k)

        def peak_result(i, peak):
            x = jnp.abs(os_[pl.ds(pl.multiple_of(i * 64, 64), 64), :])
            return jnp.maximum(peak, jnp.max(x.reshape(8, 8, R), axis=0))

        peak = lax.fori_loop(0, 16, peak_result, jnp.zeros((8, R), F32))
        log_scale = scale_of(jnp.max(peak, axis=0, keepdims=True))
        eo[k] = log_scale
        share_lines(eo.at[k], reo.at[k], 2 + k)
        inverse = jnp.exp2(-log_scale)

        def encode_result(i, carry):
            x = encode(os_[pl.ds(pl.multiple_of(i * 64, 64), 64), :], inverse)
            so[k, pl.ds(i * 4, 4)] = x.reshape(4, 16, R).astype(BF16)
            return carry

        lax.fori_loop(0, 16, encode_result, 0, unroll=2)
        send_all([(whole(so.at[k]), whole(ro.at[k]), 4 + k)])
        ro[k, s] = so[k, s]
        if k == 0:
            share_blocks(reo.at[0], 2)

    for copy in query_copies:
        copy.wait()

    def turn_queries(j, carry):
        lanes = pl.ds(pl.multiple_of(j * R, R), R)
        rows = pl.ds(pl.multiple_of(j * R, R), R)
        qt[rows, :] = qr[:, lanes].astype(F32).T
        return carry

    lax.fori_loop(0, 8, turn_queries, 0)
    share_blocks(reo.at[1], 3)
    for k in range(2):
        wait_scales(reo.at[k], 2 + k)
        wait_all(ro.at[k], rsem.at[4 + k])

        def finish(i, carry):
            x = decode(ro[k, pl.ds(i * 4, 4)], reo[k, pl.ds(i * 4, 4)])
            x = jnp.concatenate([x[:, :8], x[:, 8:]], axis=2)
            rows = pl.ds(pl.multiple_of(i * 64, 64), 64)
            q = qt[rows, :].reshape(4, 16, 2 * R)
            if k == 0:
                mixed = jnp.concatenate([q[:, :8] * x, q[:, 8:]], axis=1)
                qt[rows, :] = mixed.reshape(64, 2 * R)
            else:
                mixed = jnp.concatenate([q[:, :8], q[:, 8:] * x], axis=1)
                out[rows, :] = mixed.reshape(64, 2 * R).astype(BF16)
            return carry

        lax.fori_loop(0, 16, finish, 0)

    for k in range(2):
        wait_half(sh, k, ssem.at[k])
        wait_half(sg, k, ssem.at[2 + k])
        wait_all(so.at[k], ssem.at[4 + k])
    for i, rows in enumerate((reh, reg, reo.at[0], reo.at[1])):
        wait_rows(rows, 7, scsend.at[2 * i])
        wait_rows(rows, 56, scsend.at[2 * i + 1])


def body(streams, filter_taps, skip_gain):
    mats, twist = tables()
    streams = jnp.transpose(streams, (1, 0, 2))
    any_spec = pl.BlockSpec(memory_space=pltpu.HBM)
    dma = pltpu.SemaphoreType.DMA
    vm = pltpu.VMEM
    scratch = [
        vm((3, 64, 4096), BF16),
        vm((1024, 256), F32),
        vm((64, 4096), F32),
        vm((64, 4096), BF16),
        vm((256, 1024), BF16),
        vm((1, R), F32),
        vm((4, 1, R), F32),
        vm((256, 1024), BF16),
        vm((1024, 256), F32),
        vm((64, 32, R), BF16),
        vm((64, 32, R), BF16),
        vm((1, R), F32),
        vm((64, 1, R), F32),
        vm((64, 32, R), BF16),
        vm((64, 32, R), BF16),
        vm((1, R), F32),
        vm((64, 1, R), F32),
        vm((2, 64, 16, R), BF16),
        vm((2, 64, 16, R), BF16),
        vm((2, 1, R), F32),
        vm((2, 64, 1, R), F32),
        vm((2, 4, 2 * R, 2 * R), F32),
        vm((1032, R), F32),
        vm((1032, R), F32),
        vm((2, R, R), F32),
        [vm(m.shape, BF16) for m in mats],
        vm((3 * R, 8 * R), BF16),
        vm((2 * R, 8 * R), F32),
        vm((8 * R, 6 * R), BF16),
        vm((6 * R, 8 * R), BF16),
        dma((7,)),
        dma((3,)),
        dma((3,)),
        dma((3,)),
        dma((3,)),
        dma((3,)),
        dma((3,)),
        dma((6,)),
        dma((6,)),
        dma((8,)),
        dma((8,)),
    ]
    return pl.pallas_call(
        kernel,
        out_shape=pltpu.VMEM((1024, 256), BF16),
        in_specs=[any_spec, any_spec, pl.BlockSpec(memory_space=pltpu.SMEM)] + [any_spec] * 5,
        out_specs=pl.BlockSpec(memory_space=pltpu.VMEM),
        scratch_shapes=scratch,
        compiler_params=pltpu.CompilerParams(
            collective_id=0, has_side_effects=True, vmem_limit_bytes=63 * 1024 * 1024
        ),
    )(streams, filter_taps, skip_gain, *[jnp.asarray(m) for m in mats], jnp.asarray(twist))


def solution(mesh):
    placed = (P(("seq", "ch"), None, None), P("ch", "seq"), P("ch"))
    return jax.shard_map(
        body, mesh=mesh, in_specs=placed, out_specs=P("ch", "seq"), check_vma=False
    )
```
